32 devices in a mesh: dp: 16 (over z, x, core), seq: 2 (over y).
Axes of the slice: x: 2, y: 2, z: 4, core: 2. Of those that a mesh axis runs over, the one named last changes fastest.
Arguments:
- features: bfloat16 [16, 1024, 768], P('dp', 'seq'), may hold values from -2.5 to 2.5
- w_first: bfloat16 [2304, 768], P('dp'), may hold values from -0.125 to 0.125
- w_second: bfloat16 [2304, 768], P('dp'), may hold values from -0.125 to 0.125
- cotangent: bfloat16 [16, 1024, 768], P('dp', 'seq'), may hold values from -2.5 to 2.5
Outputs:
- tower_out: bfloat16 [16, 1024, 768], P('dp', 'seq')
- grad_input: bfloat16 [16, 1024, 768], P('dp', 'seq')
- grad_first: float32 [2304, 768], P('dp')
- grad_second: float32 [2304, 768], P('dp')
The draws below stay inside these ranges and needn't reach their ends.
All inputs are finite; a program needn't handle non-finite values.
Results may differ from the reference program's by a relative error of at most 0.014.
Values may be sent and summed in bfloat16 or wider, within the bound.
No kernel may reach another device: no remote copies, remote signals or barrier semaphores. Data moves between devices by JAX's collectives and lax.ppermute only.
A program may use at most 128 MiB of HBM per device.

```python
import math
import jax
import jax.numpy as jnp
from jax import lax

C = 768
LENGTH = 1024
SEQS = 16


def shard_levels(stream_key, extent, split, low, top_value):
    loudness, own = 1.0, jax.random.fold_in(stream_key, 6)
    for dim, blocks in split:
        draws = jnp.exp(jax.random.uniform(jax.random.fold_in(own, dim), (blocks,), jnp.float32, low / len(split), top_value / len(split)))
        loudness = loudness * jnp.repeat(draws, extent[dim] // blocks).reshape([-1 if axis == dim else 1 for axis in range(len(extent))])
    return loudness


def noise(key, dims, deviation, bound, cuts=(), held_as=jnp.bfloat16):
    values = deviation * jax.random.normal(key, dims, jnp.float32)
    if cuts:
        values = values * shard_levels(key, dims, cuts, -0.22, 0.18)
    return jnp.clip(values, -bound, bound).astype(held_as)


def setup_inputs(seed: int = 0) -> dict:
    seeds = jax.random.split(jax.random.key(seed), 5)
    features = noise(seeds[0], (SEQS, LENGTH, C), 0.5, 2.5, ((0, 16), (1, 2)))
    w_first = noise(seeds[1], (3 * C, C), (3 * C) ** -0.5, 0.125, ((0, 16),))
    w_second = noise(seeds[2], (3 * C, C), (3 * C) ** -0.5, 0.125, ((0, 16),))
    cotangent = noise(seeds[3], (SEQS, LENGTH, C), 0.5, 2.5, ((0, 16), (1, 2)))
    return dict(features=features, w_first=w_first, w_second=w_second, cotangent=cotangent)


def gelu_value(values):
    return values * 0.5 * (1.0 + lax.erf(values * 0.7071067811865476))

def gelu_slope(values):
    cumulative = 0.5 * (1.0 + lax.erf(values * 0.7071067811865476))
    density = jnp.exp(-0.5 * values * values) * 0.3989422804014327
    return cumulative + values * density

def stack_taps(padded, dilation, row_count):
    return jnp.concatenate([padded[tap_index * dilation:tap_index * dilation + row_count] for tap_index in range(3)], axis=1)

def spread_taps(product, dilation, row_count, channels):
    summed = product[2 * dilation:2 * dilation + row_count, 0:channels]
    for tap_index in (1, 2):
        offset = (2 - tap_index) * dilation
        summed = summed + product[offset:offset + row_count, tap_index * channels:(tap_index + 1) * channels]
    return summed

def one_sequence(source, upstream, w_first, w_second, grad_scale):
    row_count = source.shape[0]
    channels = source.shape[1]
    f32 = jnp.float32
    act_first = gelu_value(source.astype(f32)).astype(jnp.bfloat16)
    stack_first = stack_taps(jnp.pad(act_first, ((4, 4), (0, 0))), 4, row_count)
    hidden = (source.astype(f32) + jnp.dot(stack_first, w_first, preferred_element_type=f32)).astype(jnp.bfloat16)
    act_second = gelu_value(hidden.astype(f32)).astype(jnp.bfloat16)
    stack_second = stack_taps(jnp.pad(act_second, ((8, 8), (0, 0))), 8, row_count)
    tower = (hidden.astype(f32) + jnp.dot(stack_second, w_second, preferred_element_type=f32)).astype(jnp.bfloat16)
    grad_second = jnp.dot(stack_second.T, upstream, preferred_element_type=f32) * grad_scale
    product = jnp.dot(jnp.pad(upstream, ((8, 8), (0, 0))), w_second.T, preferred_element_type=f32)
    grad_hidden = (upstream.astype(f32) + spread_taps(product, 8, row_count, channels) * gelu_slope(hidden.astype(f32))).astype(jnp.bfloat16)
    grad_first = jnp.dot(stack_first.T, grad_hidden, preferred_element_type=f32) * grad_scale
    product = jnp.dot(jnp.pad(grad_hidden, ((4, 4), (0, 0))), w_first.T, preferred_element_type=f32)
    grad_input = (grad_hidden.astype(f32) + spread_taps(product, 4, row_count, channels) * gelu_slope(source.astype(f32))).astype(jnp.bfloat16)
    return (tower, grad_input, grad_first, grad_second)

def reference(features, w_first, w_second, cotangent):
    grad_scale = 1.0 / math.sqrt(SEQS * LENGTH)

    def advance(carry, sequence_pair):
        tower, grad_input, grad_first, grad_second = one_sequence(sequence_pair[0], sequence_pair[1], w_first, w_second, grad_scale)
        return ((carry[0] + grad_first, carry[1] + grad_second), (tower, grad_input))
    empty_grad = jnp.zeros(w_first.shape, jnp.float32)
    (total_first, total_second), (tower_rows, input_rows) = lax.scan(advance, (empty_grad, empty_grad), (features, cotangent))
    return (tower_rows, input_rows, total_first, total_second)
```

```python
import math

import jax
import jax.numpy as jnp
from jax import lax
from jax.sharding import PartitionSpec as P

F32 = jnp.float32
BF16 = jnp.bfloat16
HALO = 16
EDGE = 8


def gelu_value(values):
    return values * 0.5 * (1.0 + lax.erf(values * 0.7071067811865476))


def gelu_slope(values):
    cumulative = 0.5 * (1.0 + lax.erf(values * 0.7071067811865476))
    density = jnp.exp(-0.5 * values * values) * 0.3989422804014327
    return cumulative + values * density


def after(value, *others):
    return lax.optimization_barrier((value,) + others)[0]


def shards(features, w_first, w_second, cotangent):
    parts = lax.axis_size("dp")
    seqs = lax.axis_size("seq")
    place, me_y = lax.axis_index("dp"), lax.axis_index("seq")
    depth = parts // 4
    core, me_x, me_z = place % 2, (place // 2) % 2, place // 4
    h = me_y % 2
    rows, channels = features.shape[1], features.shape[2]
    block = w_first.shape[0]
    half = channels // 2
    grad_scale = 1.0 / math.sqrt(rows * seqs * parts)

    core_pairs = [(i, i ^ 1) for i in range(parts)]
    x_pairs = [(i, i ^ 2) for i in range(parts)]
    y_pairs = [(i, i ^ 1) for i in range(seqs)]

    def turn(step):
        return [(i, (i - 4 * step) % parts) for i in range(parts)]

    def by_core(mine, theirs, axis):
        first = jnp.where(core == 0, mine, theirs)
        second = jnp.where(core == 0, theirs, mine)
        return jnp.concatenate([first, second], axis=axis)

    def half_of(array, index, axis):
        return lax.dynamic_slice_in_dim(array, index * half, half, axis=axis)

    def take(array, index, axis):
        return lax.dynamic_index_in_dim(array, index, axis, keepdims=False)

    both = jnp.stack([w_first, w_second])
    given = lax.ppermute(half_of(both, 1 - core, 2), "dp", core_pairs)
    kept = half_of(both, core, 2)
    pair = jnp.stack(
        [jnp.where(core == 0, kept, given), jnp.where(core == 0, given, kept)], axis=1
    )

    joined = jnp.concatenate([features[0], cotangent[0]], axis=1)
    if seqs == 2:
        rim = jnp.where(h == 0, joined[rows - HALO :], joined[:HALO])
        rim = lax.ppermute(rim, "seq", y_pairs)
        none = jnp.zeros_like(rim)
        low, high = jnp.where(h == 0, none, rim), jnp.where(h == 0, rim, none)
    else:
        onward = [(i, i + 1) for i in range(seqs - 1)]
        back = [(i + 1, i) for i in range(seqs - 1)]
        low = lax.ppermute(joined[rows - HALO :], "seq", onward)
        high = lax.ppermute(joined[:HALO], "seq", back)

    def gather(which, x_pair, *others):
        piece = after(lax.dynamic_index_in_dim(pair[which], h, 0, keepdims=False), *others)
        turned = jnp.stack(
            [lax.ppermute(piece, "dp", turn(step)) for step in range(1, depth)]
        )
        from_x = lax.ppermute(turned, "dp", x_pairs)
        from_y = lax.ppermute(turned, "seq", y_pairs)
        by_y = lax.ppermute(from_x[: depth // 2], "seq", y_pairs)
        by_x = lax.ppermute(from_y[depth // 2 :], "dp", x_pairs)

        return pair[which], x_pair[which], turned, from_x, from_y, by_y, by_x

    def assemble(own, across, turned, from_x, from_y, by_y, by_x):
        both_in = jnp.concatenate([by_y, by_x], axis=0)

        def on(flag, here, there, axis):
            return jnp.stack(
                [jnp.where(flag == 0, here, there), jnp.where(flag == 0, there, here)], axis=axis
            )

        near, far = on(h, turned, from_y, 1), on(h, from_x, both_in, 1)
        near = jnp.concatenate([own[None], near], axis=0)
        far = jnp.concatenate([across[None], far], axis=0)
        lines = on(me_x, near, far, 1)
        lines = jnp.concatenate([lines, lines], axis=0)
        lines = lax.dynamic_slice_in_dim(lines, (depth - me_z) % depth, depth, axis=0)
        return lines.reshape(parts * block, half)

    x_pair = lax.ppermute(after(pair, low, high), "dp", x_pairs)
    first_pieces = gather(0, x_pair, low, high)
    second_pieces = gather(1, x_pair, first_pieces[2])

    extended = after(jnp.concatenate([low, joined, high], axis=0), first_pieces[2])
    partner = lax.ppermute(extended, "dp", core_pairs)
    pairs = jnp.stack([extended, partner])
    features_two, cot_two = pairs[..., :channels], pairs[..., channels:]
    act_first = gelu_value(features_two.astype(F32)).astype(BF16)
    wide = rows + 2 * EDGE

    def shifted(array, offset, count):
        return lax.slice_in_dim(array, offset, offset + count, axis=1)

    stack_first = jnp.concatenate(
        [shifted(act_first, HALO - EDGE + (tap - 1) * 4, wide) for tap in range(3)], axis=2
    )
    cot_halves = [half_of(cot_two, core, 2), half_of(cot_two, 1 - core, 2)]
    stack_cot = jnp.concatenate(
        [
            shifted(side, HALO - EDGE - (tap - 1) * 8, wide)
            for tap in range(3)
            for side in cot_halves
        ],
        axis=2,
    )
    cot_base = shifted(cot_halves[0], HALO - EDGE, wide)
    row = lax.broadcasted_iota(jnp.int32, (1, wide, 1), 1)
    valid = (row >= jnp.where(me_y == 0, EDGE, 0)) & (
        row < jnp.where(me_y == seqs - 1, wide - EDGE, wide)
    )
    slope_first = gelu_slope(features[0].astype(F32))

    first_base = shifted(half_of(features_two, core, 2), HALO - EDGE, wide)
    first_mine = assemble(*first_pieces)
    first_theirs = lax.ppermute(first_mine, "dp", core_pairs)
    hidden = (
        first_base.astype(F32) + jnp.dot(stack_first, first_mine, preferred_element_type=F32)
    ).astype(BF16)
    act_mine = jnp.where(valid, gelu_value(hidden.astype(F32)), 0.0).astype(BF16)
    act_theirs = lax.ppermute(act_mine, "dp", core_pairs)[::-1]
    act_second = by_core(act_mine, act_theirs, 2)
    stack_second = jnp.concatenate(
        [shifted(act_second, EDGE + (tap - 1) * 8, rows) for tap in range(3)], axis=2
    )

    def gradient(stacked, upstream):
        return (
            lax.dot_general(
                stacked.reshape(2 * rows, 3 * channels),
                upstream.reshape(2 * rows, half),
                (((0,), (0,)), ((), ())),
                preferred_element_type=F32,
            )
            * grad_scale
        ).astype(BF16)

    def add(left, right):
        return (left.astype(F32) + right.astype(F32)).astype(BF16)

    def plane_sum(grad):
        grad = grad.reshape(depth, 2, 2, block, half)
        cut = depth // 2
        one, two = grad[:cut], grad[cut:]
        one_in = lax.ppermute(take(one, 1 - me_x, 1), "dp", x_pairs)
        two_in = lax.ppermute(take(two, 1 - h, 2), "seq", y_pairs)
        return add(take(one, me_x, 1), one_in), add(take(two, h, 2), two_in)

    def plane_rest(one, two):
        one_in = lax.ppermute(take(one, 1 - h, 1), "seq", y_pairs)
        two_in = lax.ppermute(take(two, 1 - me_x, 1), "dp", x_pairs)
        one = add(take(one, h, 1), one_in)
        two = add(take(two, me_x, 1), two_in)
        return jnp.concatenate([one, two], axis=0)

    def line_sum(summed):
        total = take(summed, me_z, 0).astype(F32)
        for step in range(1, depth):
            out = take(summed, (me_z - step) % depth, 0)
            total = total + lax.ppermute(out, "dp", turn(step)).astype(F32)
        return total

    def finish(totals):
        if seqs > 2:
            groups = [[i for i in range(seqs) if i % 2 == k] for k in range(2)]
            totals = lax.psum(totals, "seq", axis_index_groups=groups)
        mine = totals.astype(BF16)
        theirs = lax.ppermute(mine, "seq", y_pairs)
        rows_two = jnp.stack(
            [jnp.where(h == 0, mine, theirs), jnp.where(h == 0, theirs, mine)], axis=0
        )
        kept = take(rows_two, core, 0)
        given = lax.ppermute(take(rows_two, 1 - core, 0), "dp", core_pairs)
        return by_core(kept, given, 2).astype(F32)

    grad_second = gradient(stack_second, shifted(cot_halves[0], HALO, rows))
    second_mine = assemble(*(after(piece, grad_second) for piece in second_pieces))
    second_theirs = lax.ppermute(second_mine, "dp", core_pairs)
    half_second = plane_sum(grad_second)
    plane_second = plane_rest(*half_second)

    slope = gelu_slope(hidden.astype(F32))
    blocks = jnp.stack(
        [take(side.reshape(3, 2, half, half), core, 1) for side in (second_mine, second_theirs)],
        axis=1,
    )
    spread = jnp.dot(
        after(stack_cot, *half_second),
        blocks.transpose(0, 1, 3, 2).reshape(3 * channels, half),
        preferred_element_type=F32,
    )
    grad_mine = jnp.where(valid, cot_base.astype(F32) + spread * slope, 0.0).astype(BF16)
    grad_first = gradient(shifted(stack_first, EDGE, rows), shifted(grad_mine, EDGE, rows))
    plane_first = plane_rest(*plane_sum(after(grad_first, plane_second)))

    tower_mine = (
        shifted(hidden, EDGE, rows).astype(F32)
        + jnp.dot(stack_second, second_mine, preferred_element_type=F32)
    ).astype(BF16)
    sent = jnp.concatenate([tower_mine[1], grad_mine[1]], axis=0)
    came = lax.ppermute(sent, "dp", core_pairs)
    tower = by_core(tower_mine[0], came[:rows], 1)
    grad_hidden = by_core(grad_mine[0], came[rows:], 1)

    w_first_whole = by_core(first_mine, first_theirs, 1).reshape(3, channels, channels)
    spread = None
    for tap in range(3):
        offset = EDGE - (tap - 1) * 4
        product = lax.dot_general(
            grad_hidden, w_first_whole[tap], (((1,), (1,)), ((), ())), preferred_element_type=F32
        )[offset : offset + rows]
        spread = product if spread is None else spread + product
    grad_input = (
        grad_hidden[EDGE : EDGE + rows].astype(F32) + spread * slope_first
    ).astype(BF16)

    done = finish(jnp.stack([line_sum(plane_first), line_sum(plane_second)]))
    return (tower[None], grad_input[None], done[0], done[1])


def solution(mesh):
    return jax.shard_map(
        shards,
        mesh=mesh,
        in_specs=(P("dp", "seq", None), P("dp", None), P("dp", None), P("dp", "seq", None)),
        out_specs=(P("dp", "seq", None), P("dp", "seq", None), P("dp", None), P("dp", None)),
        check_vma=False,
    )
```

```python
import math

import jax
import jax.numpy as jnp
from jax import lax
from jax.sharding import PartitionSpec as P

F32 = jnp.float32
BF16 = jnp.bfloat16
HALO = 16
EDGE = 8


def gelu_value(values):
    return values * 0.5 * (1.0 + lax.erf(values * 0.7071067811865476))


def gelu_slope(values):
    cumulative = 0.5 * (1.0 + lax.erf(values * 0.7071067811865476))
    density = jnp.exp(-0.5 * values * values) * 0.3989422804014327
    return cumulative + values * density


def together(*values):
    return lax.optimization_barrier(values)


def after(value, *others):
    return lax.optimization_barrier((value,) + others)[0]


def shards(features, w_first, w_second, cotangent):
    parts = lax.axis_size("dp")
    seqs = lax.axis_size("seq")
    place, me_y = lax.axis_index("dp"), lax.axis_index("seq")
    depth = parts // 4
    core, me_x, me_z = place % 2, (place // 2) % 2, place // 4
    h = me_y % 2
    rows, channels = features.shape[1], features.shape[2]
    block = w_first.shape[0]
    half = channels // 2
    grad_scale = 1.0 / math.sqrt(rows * seqs * parts)

    core_pairs = [(i, i ^ 1) for i in range(parts)]
    x_pairs = [(i, i ^ 2) for i in range(parts)]
    y_pairs = [(i, i ^ 1) for i in range(seqs)]
    xy_pairs = [((i ^ 2) * seqs + k, i * seqs + (k ^ 1)) for i in range(parts) for k in range(seqs)]

    def turn(step):
        return [(i, (i - 4 * step) % parts) for i in range(parts)]

    def by_core(mine, theirs, axis):
        first = jnp.where(core == 0, mine, theirs)
        second = jnp.where(core == 0, theirs, mine)
        return jnp.concatenate([first, second], axis=axis)

    def half_of(array, index, axis):
        return lax.dynamic_slice_in_dim(array, index * half, half, axis=axis)

    def take(array, index, axis):
        return lax.dynamic_index_in_dim(array, index, axis, keepdims=False)

    both = jnp.stack([w_first, w_second])
    given = lax.ppermute(half_of(both, 1 - core, 2), "dp", core_pairs)
    kept = half_of(both, core, 2)
    pair = jnp.stack(
        [jnp.where(core == 0, kept, given), jnp.where(core == 0, given, kept)], axis=1
    )

    joined = jnp.concatenate([features[0], cotangent[0]], axis=1)
    if seqs == 2:
        rim = jnp.where(h == 0, joined[rows - HALO :], joined[:HALO])
        rim = lax.ppermute(rim, "seq", y_pairs)
        none = jnp.zeros_like(rim)
        low, high = jnp.where(h == 0, none, rim), jnp.where(h == 0, rim, none)
    else:
        onward = [(i, i + 1) for i in range(seqs - 1)]
        back = [(i + 1, i) for i in range(seqs - 1)]
        low = lax.ppermute(joined[rows - HALO :], "seq", onward)
        high = lax.ppermute(joined[:HALO], "seq", back)

    def along_z(which, *others):
        piece = after(lax.dynamic_index_in_dim(pair[which], h, 0, keepdims=False), *others)
        return jnp.stack(
            together(*(lax.ppermute(piece, "dp", turn(step)) for step in range(1, depth)))
        )

    def across(turned, *others):
        given = after(turned, *others)
        return lax.ppermute(given, "dp", x_pairs), lax.ppermute(given, "seq", y_pairs)

    def corner(turned, *others):
        return lax.ppermute(after(turned, *others), ("dp", "seq"), xy_pairs)

    def assemble(own, across, turned, from_x, from_y, from_xy):
        def on(flag, here, there, axis):
            return jnp.stack(
                [jnp.where(flag == 0, here, there), jnp.where(flag == 0, there, here)], axis=axis
            )

        near, far = on(h, turned, from_y, 1), on(h, from_x, from_xy, 1)
        near = jnp.concatenate([own[None], near], axis=0)
        far = jnp.concatenate([across[None], far], axis=0)
        lines = on(me_x, near, far, 1)
        lines = jnp.concatenate([lines, lines], axis=0)
        lines = lax.dynamic_slice_in_dim(lines, (depth - me_z) % depth, depth, axis=0)
        return lines.reshape(parts * block, half)

    x_pair = lax.ppermute(after(pair, low, high), "dp", x_pairs)
    first_turned = along_z(0, low, high)
    first_across = across(first_turned)
    first_corner = corner(first_turned)
    second_turned = along_z(1, first_turned)
    second_across = across(second_turned, first_corner)

    extended = after(jnp.concatenate([low, joined, high], axis=0), first_turned)
    partner = lax.ppermute(extended, "dp", core_pairs)
    pairs = jnp.stack([extended, partner])
    features_two, cot_two = pairs[..., :channels], pairs[..., channels:]
    act_first = gelu_value(features_two.astype(F32)).astype(BF16)
    wide = rows + 2 * EDGE

    def shifted(array, offset, count):
        return lax.slice_in_dim(array, offset, offset + count, axis=1)

    stack_first = jnp.concatenate(
        [shifted(act_first, HALO - EDGE + (tap - 1) * 4, wide) for tap in range(3)], axis=2
    )
    cot_mine = half_of(cot_two, core, 2)
    cot_base = shifted(cot_mine, HALO - EDGE, wide)
    row = lax.broadcasted_iota(jnp.int32, (1, wide, 1), 1)
    valid = (row >= jnp.where(me_y == 0, EDGE, 0)) & (
        row < jnp.where(me_y == seqs - 1, wide - EDGE, wide)
    )
    slope_first = gelu_slope(features[0].astype(F32))

    first_base = shifted(half_of(features_two, core, 2), HALO - EDGE, wide)
    first_mine = assemble(pair[0], x_pair[0], first_turned, *first_across, first_corner)
    first_theirs = lax.ppermute(first_mine, "dp", core_pairs)
    hidden = (
        first_base.astype(F32) + jnp.dot(stack_first, first_mine, preferred_element_type=F32)
    ).astype(BF16)
    act_mine = jnp.where(valid, gelu_value(hidden.astype(F32)), 0.0).astype(BF16)
    second_corner = corner(second_turned, act_mine)
    act_theirs = lax.ppermute(act_mine, "dp", core_pairs)[::-1]
    act_second = by_core(act_mine, act_theirs, 2)
    stack_second = jnp.concatenate(
        [shifted(act_second, EDGE + (tap - 1) * 8, rows) for tap in range(3)], axis=2
    )

    def gradient(stacked, upstream):
        return (
            lax.dot_general(
                stacked.reshape(2 * rows, 3 * channels),
                upstream.reshape(2 * rows, half),
                (((0,), (0,)), ((), ())),
                preferred_element_type=F32,
            )
            * grad_scale
        ).astype(BF16)

    def add(left, right):
        return (left.astype(F32) + right.astype(F32)).astype(BF16)

    def plane_sum(grad):
        grad = grad.reshape(depth, 2, 2, block, half)
        cut = depth // 2
        one, two = grad[:cut], grad[cut:]
        one_out, two_out = together(take(one, 1 - me_x, 1), take(two, 1 - h, 2))
        one_in = lax.ppermute(one_out, "dp", x_pairs)
        two_in = lax.ppermute(two_out, "seq", y_pairs)
        one_in, two_in = together(one_in, two_in)
        return add(take(one, me_x, 1), one_in), add(take(two, h, 2), two_in)

    def plane_rest(one, two):
        one_out, two_out = together(take(one, 1 - h, 1), take(two, 1 - me_x, 1))
        one_in = lax.ppermute(one_out, "seq", y_pairs)
        two_in = lax.ppermute(two_out, "dp", x_pairs)
        one_in, two_in = together(one_in, two_in)
        one = add(take(one, h, 1), one_in)
        two = add(take(two, me_x, 1), two_in)
        return jnp.concatenate([one, two], axis=0)

    def line_sum(summed):
        outs = together(
            *(take(summed, (me_z - step) % depth, 0) for step in range(1, depth))
        )
        total = take(summed, me_z, 0).astype(F32)
        for step, out in enumerate(outs, 1):
            total = total + lax.ppermute(out, "dp", turn(step)).astype(F32)
        return total

    def finish(totals):
        if seqs > 2:
            groups = [[i for i in range(seqs) if i % 2 == k] for k in range(2)]
            totals = lax.psum(totals, "seq", axis_index_groups=groups)
        mine = totals.astype(BF16)
        theirs = lax.ppermute(mine, "seq", y_pairs)
        rows_two = jnp.stack(
            [jnp.where(h == 0, mine, theirs), jnp.where(h == 0, theirs, mine)], axis=0
        )
        kept = take(rows_two, core, 0)
        given = lax.ppermute(take(rows_two, 1 - core, 0), "dp", core_pairs)
        return by_core(kept, given, 2).astype(F32)

    grad_second = gradient(stack_second, shifted(cot_mine, HALO, rows))
    second_pieces = pair[1], x_pair[1], second_turned, *second_across, second_corner
    second_mine = assemble(*(after(piece, grad_second) for piece in second_pieces))
    second_theirs = lax.ppermute(second_mine, "dp", core_pairs)
    half_second = plane_sum(grad_second)
    plane_second = plane_rest(*half_second)

    slope = gelu_slope(hidden.astype(F32))
    mine, theirs = (
        take(side.reshape(3, 2, half, half), core, 1) for side in (second_mine, second_theirs)
    )
    product = lax.dot_general(
        after(cot_two, *half_second),
        by_core(mine, theirs, 2).reshape(3 * half, channels),
        (((2,), (1,)), ((), ())),
        preferred_element_type=F32,
    )
    spread = None
    for tap in range(3):
        part = shifted(product[..., tap * half : (tap + 1) * half], HALO - EDGE - (tap - 1) * 8, wide)
        spread = part if spread is None else spread + part
    grad_mine = jnp.where(valid, cot_base.astype(F32) + spread * slope, 0.0).astype(BF16)
    grad_first = gradient(shifted(stack_first, EDGE, rows), shifted(grad_mine, EDGE, rows))
    plane_first = plane_rest(*plane_sum(after(grad_first, plane_second)))

    tower_mine = (
        shifted(hidden, EDGE, rows).astype(F32)
        + jnp.dot(stack_second, second_mine, preferred_element_type=F32)
    ).astype(BF16)
    sent = jnp.concatenate([tower_mine[1], grad_mine[1]], axis=0)
    came = lax.ppermute(sent, "dp", core_pairs)
    tower = by_core(tower_mine[0], came[:rows], 1)
    grad_hidden = by_core(grad_mine[0], came[rows:], 1)

    w_first_whole = by_core(first_mine, first_theirs, 1).reshape(3, channels, channels)
    spread = None
    for tap in range(3):
        offset = EDGE - (tap - 1) * 4
        product = lax.dot_general(
            grad_hidden, w_first_whole[tap], (((1,), (1,)), ((), ())), preferred_element_type=F32
        )[offset : offset + rows]
        spread = product if spread is None else spread + product
    grad_input = (
        grad_hidden[EDGE : EDGE + rows].astype(F32) + spread * slope_first
    ).astype(BF16)

    done = finish(jnp.stack([line_sum(plane_first), line_sum(plane_second)]))
    return (tower[None], grad_input[None], done[0], done[1])


def solution(mesh):
    return jax.shard_map(
        shards,
        mesh=mesh,
        in_specs=(P("dp", "seq", None), P("dp", None), P("dp", None), P("dp", "seq", None)),
        out_specs=(P("dp", "seq", None), P("dp", "seq", None), P("dp", None), P("dp", None)),
        check_vma=False,
    )
```

```python
import math

import jax
import jax.numpy as jnp
from jax import lax
from jax.sharding import PartitionSpec as P

F32 = jnp.float32
BF16 = jnp.bfloat16
HALO = 16
EDGE = 8


def gelu_value(values):
    return values * 0.5 * (1.0 + lax.erf(values * 0.7071067811865476))


def gelu_slope(values):
    cumulative = 0.5 * (1.0 + lax.erf(values * 0.7071067811865476))
    density = jnp.exp(-0.5 * values * values) * 0.3989422804014327
    return cumulative + values * density


def together(*values):
    return lax.optimization_barrier(values)


def after(value, *others):
    return lax.optimization_barrier((value,) + others)[0]


def shards(features, w_first, w_second, cotangent):
    parts = lax.axis_size("dp")
    seqs = lax.axis_size("seq")
    place, me_y = lax.axis_index("dp"), lax.axis_index("seq")
    depth = parts // 4
    core, me_x, me_z = place % 2, (place // 2) % 2, place // 4
    h = me_y % 2
    rows, channels = features.shape[1], features.shape[2]
    block = w_first.shape[0]
    half = channels // 2
    grad_scale = 1.0 / math.sqrt(rows * seqs * parts)

    core_pairs = [(i, i ^ 1) for i in range(parts)]
    x_pairs = [(i, i ^ 2) for i in range(parts)]
    y_pairs = [(i, i ^ 1) for i in range(seqs)]
    xy_pairs = [((i ^ 2) * seqs + k, i * seqs + (k ^ 1)) for i in range(parts) for k in range(seqs)]

    def turn(step):
        return [(i, (i - 4 * step) % parts) for i in range(parts)]

    def by_core(mine, theirs, axis):
        first = jnp.where(core == 0, mine, theirs)
        second = jnp.where(core == 0, theirs, mine)
        return jnp.concatenate([first, second], axis=axis)

    def half_of(array, index, axis):
        return lax.dynamic_slice_in_dim(array, index * half, half, axis=axis)

    def take(array, index, axis):
        return lax.dynamic_index_in_dim(array, index, axis, keepdims=False)

    both = jnp.stack([w_first, w_second])
    given = lax.ppermute(half_of(both, 1 - core, 2), "dp", core_pairs)
    kept = half_of(both, core, 2)
    pair = jnp.stack(
        [jnp.where(core == 0, kept, given), jnp.where(core == 0, given, kept)], axis=1
    )

    joined = jnp.concatenate([features[0], cotangent[0]], axis=1)
    if seqs == 2:
        rim = jnp.where(h == 0, joined[rows - HALO :], joined[:HALO])
        rim = lax.ppermute(rim, "seq", y_pairs)
        none = jnp.zeros_like(rim)
        low, high = jnp.where(h == 0, none, rim), jnp.where(h == 0, rim, none)
    else:
        onward = [(i, i + 1) for i in range(seqs - 1)]
        back = [(i + 1, i) for i in range(seqs - 1)]
        low = lax.ppermute(joined[rows - HALO :], "seq", onward)
        high = lax.ppermute(joined[:HALO], "seq", back)

    def along_z(which, *others):
        piece = after(lax.dynamic_index_in_dim(pair[which], h, 0, keepdims=False), *others)
        return jnp.stack(
            together(*(lax.ppermute(piece, "dp", turn(step)) for step in range(1, depth)))
        )

    def across(turned, *others):
        given = after(turned, *others)
        return lax.ppermute(given, "dp", x_pairs), lax.ppermute(given, "seq", y_pairs)

    def corner(turned, *others):
        return lax.ppermute(after(turned, *others), ("dp", "seq"), xy_pairs)

    def assemble(own, across, turned, from_x, from_y, from_xy):
        def on(flag, here, there, axis):
            return jnp.stack(
                [jnp.where(flag == 0, here, there), jnp.where(flag == 0, there, here)], axis=axis
            )

        near, far = on(h, turned, from_y, 1), on(h, from_x, from_xy, 1)
        near = jnp.concatenate([own[None], near], axis=0)
        far = jnp.concatenate([across[None], far], axis=0)
        lines = on(me_x, near, far, 1)
        lines = jnp.concatenate([lines, lines], axis=0)
        lines = lax.dynamic_slice_in_dim(lines, (depth - me_z) % depth, depth, axis=0)
        return lines.reshape(parts * block, half)

    x_pair = lax.ppermute(after(pair, low, high), "dp", x_pairs)
    first_turned, x_pair = together(along_z(0, low, high), x_pair)
    first_across = across(first_turned)
    first_corner = corner(first_turned)

    extended = after(jnp.concatenate([low, joined, high], axis=0), first_turned)
    partner = lax.ppermute(extended, "dp", core_pairs)
    pairs = jnp.stack([extended, partner])
    features_two, cot_two = pairs[..., :channels], pairs[..., channels:]
    act_first = gelu_value(features_two.astype(F32)).astype(BF16)
    second_turned = along_z(1)
    second_across = across(second_turned, first_corner, *first_across)
    second_corner = corner(second_turned, first_corner, *first_across)
    second_pieces = pair[1], x_pair[1], second_turned, *second_across, second_corner
    wide = rows + 2 * EDGE

    def shifted(array, offset, count):
        return lax.slice_in_dim(array, offset, offset + count, axis=1)

    stack_first = jnp.concatenate(
        [shifted(act_first, HALO - EDGE + (tap - 1) * 4, wide) for tap in range(3)], axis=2
    )
    cot_mine = half_of(cot_two, core, 2)
    cot_base = shifted(cot_mine, HALO - EDGE, wide)
    row = lax.broadcasted_iota(jnp.int32, (1, wide, 1), 1)
    valid = (row >= jnp.where(me_y == 0, EDGE, 0)) & (
        row < jnp.where(me_y == seqs - 1, wide - EDGE, wide)
    )
    slope_first = gelu_slope(features[0].astype(F32))

    first_base = shifted(half_of(features_two, core, 2), HALO - EDGE, wide)
    first_pieces = pair[0], x_pair[0], first_turned, *first_across, first_corner
    first_mine = assemble(*together(*first_pieces, second_turned)[:-1])
    first_theirs = lax.ppermute(first_mine, "dp", core_pairs)
    hidden = (
        first_base.astype(F32) + jnp.dot(stack_first, first_mine, preferred_element_type=F32)
    ).astype(BF16)
    act_mine = jnp.where(valid, gelu_value(hidden.astype(F32)), 0.0).astype(BF16)
    second_mine = assemble(*second_pieces)
    second_theirs = lax.ppermute(second_mine, "dp", core_pairs)
    act_theirs = lax.ppermute(act_mine, "dp", core_pairs)[::-1]
    act_second = by_core(act_mine, act_theirs, 2)
    stack_second = jnp.concatenate(
        [shifted(act_second, EDGE + (tap - 1) * 8, rows) for tap in range(3)], axis=2
    )

    def gradient(stacked, upstream):
        return (
            lax.dot_general(
                stacked.reshape(2 * rows, 3 * channels),
                upstream.reshape(2 * rows, half),
                (((0,), (0,)), ((), ())),
                preferred_element_type=F32,
            )
            * grad_scale
        ).astype(BF16)

    def add(left, right):
        return (left.astype(F32) + right.astype(F32)).astype(BF16)

    cut = depth // 2

    def first_out(grad):
        grad = grad.reshape(depth, 2, 2, block, half)
        return take(grad[:cut], 1 - me_x, 1), take(grad[cut:], 1 - h, 2)

    def first_sum(grad, one_in, two_in):
        grad = grad.reshape(depth, 2, 2, block, half)
        return add(take(grad[:cut], me_x, 1), one_in), add(take(grad[cut:], h, 2), two_in)

    def second_out(one, two):
        return take(one, 1 - h, 1), take(two, 1 - me_x, 1)

    def second_sum(one, two, one_in, two_in):
        one, two = add(take(one, h, 1), one_in), add(take(two, me_x, 1), two_in)
        return jnp.concatenate([one, two], axis=0)

    def line_out(summed):
        return tuple(take(summed, (me_z - step) % depth, 0) for step in range(1, depth))

    def line_sum(summed, came):
        total = take(summed, me_z, 0).astype(F32)
        for part in came:
            total = total + part.astype(F32)
        return total

    def by_x(array):
        return lax.ppermute(array, "dp", x_pairs)

    def by_y(array):
        return lax.ppermute(array, "seq", y_pairs)

    def by_z(outs):
        return tuple(lax.ppermute(out, "dp", turn(step)) for step, out in enumerate(outs, 1))

    def across_y(total):
        if seqs > 2:
            groups = [[i for i in range(seqs) if i % 2 == k] for k in range(2)]
            total = lax.psum(total, "seq", axis_index_groups=groups)
        mine = total.astype(BF16)
        return mine, by_y(mine)

    def finish(*pieces):
        mine, theirs = jnp.stack(pieces[::2]), jnp.stack(pieces[1::2])
        same = h == core
        kept = jnp.where(same, mine, theirs)
        given = lax.ppermute(jnp.where(same, theirs, mine), "dp", core_pairs)
        return by_core(kept, given, 2).astype(F32)

    slope = gelu_slope(hidden.astype(F32))
    mine, theirs = (
        take(side.reshape(3, 2, half, half), core, 1) for side in (second_mine, second_theirs)
    )
    product = lax.dot_general(
        cot_two,
        by_core(mine, theirs, 2).reshape(3 * half, channels),
        (((2,), (1,)), ((), ())),
        preferred_element_type=F32,
    )
    spread = None
    for tap in range(3):
        part = shifted(product[..., tap * half : (tap + 1) * half], HALO - EDGE - (tap - 1) * 8, wide)
        spread = part if spread is None else spread + part
    grad_mine = jnp.where(valid, cot_base.astype(F32) + spread * slope, 0.0).astype(BF16)
    grad_first = gradient(
        shifted(stack_first, EDGE, rows), shifted(grad_mine, EDGE, rows)
    )
    x_out, y_out = together(*first_out(grad_first))
    first_came = by_x(x_out), by_y(y_out)
    grad_second = gradient(stack_second, shifted(cot_mine, HALO, rows))

    tower_mine = (
        shifted(hidden, EDGE, rows).astype(F32)
        + jnp.dot(stack_second, second_mine, preferred_element_type=F32)
    ).astype(BF16)
    sent = jnp.concatenate([tower_mine[1], grad_mine[1]], axis=0)
    sent, grad_second = together(sent, grad_second)
    came = lax.ppermute(sent, "dp", core_pairs)
    came, *first_came = together(came, *first_came)
    half_first = first_sum(grad_first, *first_came)
    y_out, x_out, x_next, y_next = together(*second_out(*half_first), *first_out(grad_second))
    y_in, x_in, x_come, y_come = together(by_y(y_out), by_x(x_out), by_x(x_next), by_y(y_next))
    plane_first = second_sum(*half_first, y_in, x_in)
    half_second = first_sum(grad_second, x_come, y_come)
    y_out, x_out, *outs = together(*second_out(*half_second), *line_out(plane_first))
    y_in, x_in, *line_first = together(by_y(y_out), by_x(x_out), *by_z(outs))
    plane_second = second_sum(*half_second, y_in, x_in)
    total_first = line_sum(plane_first, line_first)
    total_first, *outs = together(total_first, *line_out(plane_second))
    line_second = by_z(outs)
    tower = by_core(tower_mine[0], came[:rows], 1)
    grad_hidden = by_core(grad_mine[0], came[rows:], 1)

    w_first_whole = by_core(first_mine, first_theirs, 1).reshape(3, channels, channels)
    spread = None
    for tap in range(3):
        offset = EDGE - (tap - 1) * 4
        product = lax.dot_general(
            grad_hidden, w_first_whole[tap], (((1,), (1,)), ((), ())), preferred_element_type=F32
        )[offset : offset + rows]
        spread = product if spread is None else spread + product
    grad_input = (
        grad_hidden[EDGE : EDGE + rows].astype(F32) + spread * slope_first
    ).astype(BF16)

    total_first, grad_input = together(total_first, grad_input)
    across_first = across_y(total_first)
    across_second = across_y(line_sum(plane_second, line_second))
    done = finish(*together(*across_first, *across_second))
    return (tower[None], grad_input[None], done[0], done[1])


def solution(mesh):
    return jax.shard_map(
        shards,
        mesh=mesh,
        in_specs=(P("dp", "seq", None), P("dp", None), P("dp", None), P("dp", "seq", None)),
        out_specs=(P("dp", "seq", None), P("dp", "seq", None), P("dp", None), P("dp", None)),
        check_vma=False,
    )
```

```python
import math

import jax
import jax.numpy as jnp
from jax import lax
from jax.sharding import PartitionSpec as P

F32 = jnp.float32
BF16 = jnp.bfloat16
HALO = 16
EDGE = 8


def gelu_value(values):
    return values * 0.5 * (1.0 + lax.erf(values * 0.7071067811865476))


def gelu_slope(values):
    cumulative = 0.5 * (1.0 + lax.erf(values * 0.7071067811865476))
    density = jnp.exp(-0.5 * values * values) * 0.3989422804014327
    return cumulative + values * density


def together(*values):
    return lax.optimization_barrier(values)


def after(value, *others):
    return lax.optimization_barrier((value,) + others)[0]


def shards(features, w_first, w_second, cotangent):
    parts = lax.axis_size("dp")
    seqs = lax.axis_size("seq")
    place, me_y = lax.axis_index("dp"), lax.axis_index("seq")
    depth = parts // 4
    core, me_x, me_z = place % 2, (place // 2) % 2, place // 4
    h = me_y % 2
    rows, channels = features.shape[1], features.shape[2]
    block = w_first.shape[0]
    half = channels // 2
    grad_scale = 1.0 / math.sqrt(rows * seqs * parts)

    core_pairs = [(i, i ^ 1) for i in range(parts)]
    x_pairs = [(i, i ^ 2) for i in range(parts)]
    y_pairs = [(i, i ^ 1) for i in range(seqs)]

    def turn(step):
        return [(i, (i - 4 * step) % parts) for i in range(parts)]

    def by_core(mine, theirs, axis):
        first = jnp.where(core == 0, mine, theirs)
        second = jnp.where(core == 0, theirs, mine)
        return jnp.concatenate([first, second], axis=axis)

    def half_of(array, index, axis):
        return lax.dynamic_slice_in_dim(array, index * half, half, axis=axis)

    def take(array, index, axis):
        return lax.dynamic_index_in_dim(array, index, axis, keepdims=False)

    both = jnp.stack([w_first, w_second])
    given = lax.ppermute(half_of(both, 1 - core, 2), "dp", core_pairs)
    kept = half_of(both, core, 2)
    pair = jnp.stack(
        [jnp.where(core == 0, kept, given), jnp.where(core == 0, given, kept)], axis=1
    )

    joined = jnp.concatenate([features[0], cotangent[0]], axis=1)
    joined, pair = together(joined, pair)
    if seqs == 2:
        rim = jnp.where(h == 0, joined[rows - HALO :], joined[:HALO])
        rim = lax.ppermute(rim, "seq", y_pairs)
        none = jnp.zeros_like(rim)
        low, high = jnp.where(h == 0, none, rim), jnp.where(h == 0, rim, none)
    else:
        onward = [(i, i + 1) for i in range(seqs - 1)]
        back = [(i + 1, i) for i in range(seqs - 1)]
        low = lax.ppermute(joined[rows - HALO :], "seq", onward)
        high = lax.ppermute(joined[:HALO], "seq", back)

    def by_x(array):
        return lax.ppermute(array, "dp", x_pairs)

    def by_y(array):
        return lax.ppermute(array, "seq", y_pairs)

    def by_z(outs):
        return tuple(lax.ppermute(out, "dp", turn(step)) for step, out in enumerate(outs, 1))

    def along_z(piece):
        return jnp.stack(together(*by_z([piece] * (depth - 1))))

    def assemble(own, across, turned, from_x, from_y, from_xy):
        def on(flag, here, there, axis):
            return jnp.stack(
                [jnp.where(flag == 0, here, there), jnp.where(flag == 0, there, here)], axis=axis
            )

        near, far = on(h, turned, from_y, 1), on(h, from_x, from_xy, 1)
        near = jnp.concatenate([own[None], near], axis=0)
        far = jnp.concatenate([across[None], far], axis=0)
        lines = on(me_x, near, far, 1)
        lines = jnp.concatenate([lines, lines], axis=0)
        lines = lax.dynamic_slice_in_dim(lines, (depth - me_z) % depth, depth, axis=0)
        return lines.reshape(parts * block, half)

    first_piece, second_piece = (take(pair[which], h, 0) for which in range(2))
    first_turned, x_pair = together(along_z(first_piece), by_x(pair))
    low, high, second_piece = together(low, high, second_piece)
    second_turned = along_z(second_piece)
    first_x, first_y = by_x(first_turned), by_y(first_turned)
    first_x, first_y, second_turned = together(first_x, first_y, second_turned)
    second_x, second_y = by_x(second_turned), by_y(second_turned)
    first_pieces = pair[0], x_pair[0], first_turned, first_x, first_y, by_y(first_x)
    second_pieces = pair[1], x_pair[1], second_turned, second_x, second_y, by_x(second_y)

    extended = jnp.concatenate([low, joined, high], axis=0)
    partner = lax.ppermute(extended, "dp", core_pairs)
    pairs = jnp.stack([extended, partner])
    features_two, cot_two = pairs[..., :channels], pairs[..., channels:]
    act_first = gelu_value(features_two.astype(F32)).astype(BF16)
    wide = rows + 2 * EDGE

    def shifted(array, offset, count):
        return lax.slice_in_dim(array, offset, offset + count, axis=1)

    stack_first = jnp.concatenate(
        [shifted(act_first, HALO - EDGE + (tap - 1) * 4, wide) for tap in range(3)], axis=2
    )
    cot_mine = half_of(cot_two, core, 2)
    cot_base = shifted(cot_mine, HALO - EDGE, wide)
    row = lax.broadcasted_iota(jnp.int32, (1, wide, 1), 1)
    valid = (row >= jnp.where(me_y == 0, EDGE, 0)) & (
        row < jnp.where(me_y == seqs - 1, wide - EDGE, wide)
    )
    slope_first = gelu_slope(features[0].astype(F32))

    first_base = shifted(half_of(features_two, core, 2), HALO - EDGE, wide)
    first_mine = assemble(*first_pieces)
    first_theirs = lax.ppermute(first_mine, "dp", core_pairs)
    hidden = (
        first_base.astype(F32) + jnp.dot(stack_first, first_mine, preferred_element_type=F32)
    ).astype(BF16)
    act_mine = jnp.where(valid, gelu_value(hidden.astype(F32)), 0.0).astype(BF16)
    second_mine = assemble(*second_pieces)
    second_theirs = lax.ppermute(second_mine, "dp", core_pairs)
    act_theirs = lax.ppermute(act_mine, "dp", core_pairs)[::-1]
    act_second = by_core(act_mine, act_theirs, 2)
    stack_second = jnp.concatenate(
        [shifted(act_second, EDGE + (tap - 1) * 8, rows) for tap in range(3)], axis=2
    )

    def gradient(stacked, upstream):
        return (
            lax.dot_general(
                stacked.reshape(2 * rows, 3 * channels),
                upstream.reshape(2 * rows, half),
                (((0,), (0,)), ((), ())),
                preferred_element_type=F32,
            )
            * grad_scale
        ).astype(BF16)

    def add(left, right):
        return (left.astype(F32) + right.astype(F32)).astype(BF16)

    cut = depth // 2

    def first_out(grad):
        grad = grad.reshape(depth, 2, 2, block, half)
        return take(grad[:cut], 1 - me_x, 1), take(grad[cut:], 1 - h, 2)

    def first_sum(grad, one_in, two_in):
        grad = grad.reshape(depth, 2, 2, block, half)
        return add(take(grad[:cut], me_x, 1), one_in), add(take(grad[cut:], h, 2), two_in)

    def second_out(one, two):
        return take(one, 1 - h, 1), take(two, 1 - me_x, 1)

    def second_sum(one, two, one_in, two_in):
        one, two = add(take(one, h, 1), one_in), add(take(two, me_x, 1), two_in)
        return jnp.concatenate([one, two], axis=0)

    def line_out(summed):
        return tuple(take(summed, (me_z - step) % depth, 0) for step in range(1, depth))

    def line_sum(summed, came):
        total = take(summed, me_z, 0).astype(F32)
        for part in came:
            total = total + part.astype(F32)
        return total

    def across_y(total):
        if seqs > 2:
            groups = [[i for i in range(seqs) if i % 2 == k] for k in range(2)]
            total = lax.psum(total, "seq", axis_index_groups=groups)
        mine = total.astype(BF16)
        return mine, by_y(mine)

    def finish(*pieces):
        mine, theirs = jnp.stack(pieces[::2]), jnp.stack(pieces[1::2])
        same = h == core
        kept = jnp.where(same, mine, theirs)
        given = lax.ppermute(jnp.where(same, theirs, mine), "dp", core_pairs)
        return by_core(kept, given, 2).astype(F32)

    slope = gelu_slope(hidden.astype(F32))
    mine, theirs = (
        take(side.reshape(3, 2, half, half), core, 1) for side in (second_mine, second_theirs)
    )
    product = lax.dot_general(
        cot_two,
        by_core(mine, theirs, 2).reshape(3 * half, channels),
        (((2,), (1,)), ((), ())),
        preferred_element_type=F32,
    )
    spread = None
    for tap in range(3):
        part = shifted(product[..., tap * half : (tap + 1) * half], HALO - EDGE - (tap - 1) * 8, wide)
        spread = part if spread is None else spread + part
    grad_mine = jnp.where(valid, cot_base.astype(F32) + spread * slope, 0.0).astype(BF16)
    grad_first = gradient(
        shifted(stack_first, EDGE, rows), shifted(grad_mine, EDGE, rows)
    )
    x_out, y_out = together(*first_out(grad_first))
    first_came = by_x(x_out), by_y(y_out)
    grad_second = gradient(stack_second, shifted(cot_mine, HALO, rows))

    tower_mine = (
        shifted(hidden, EDGE, rows).astype(F32)
        + jnp.dot(stack_second, second_mine, preferred_element_type=F32)
    ).astype(BF16)
    sent = jnp.concatenate([tower_mine[1], grad_mine[1]], axis=0)
    sent, grad_second = together(sent, grad_second)
    came = lax.ppermute(sent, "dp", core_pairs)
    came, *first_came = together(came, *first_came)
    half_first = first_sum(grad_first, *first_came)
    y_out, x_out, x_next, y_next = together(*second_out(*half_first), *first_out(grad_second))
    y_in, x_in, x_come, y_come = together(by_y(y_out), by_x(x_out), by_x(x_next), by_y(y_next))
    plane_first = second_sum(*half_first, y_in, x_in)
    half_second = first_sum(grad_second, x_come, y_come)
    y_out, x_out, *outs = together(*second_out(*half_second), *line_out(plane_first))
    y_in, x_in, *line_first = together(by_y(y_out), by_x(x_out), *by_z(outs))
    plane_second = second_sum(*half_second, y_in, x_in)
    total_first = line_sum(plane_first, line_first)
    total_first, *outs = together(total_first, *line_out(plane_second))
    line_second = by_z(outs)
    tower = by_core(tower_mine[0], came[:rows], 1)
    grad_hidden = by_core(grad_mine[0], came[rows:], 1)

    w_first_whole = by_core(first_mine, first_theirs, 1).reshape(3, channels, channels)
    spread = None
    for tap in range(3):
        offset = EDGE - (tap - 1) * 4
        product = lax.dot_general(
            grad_hidden, w_first_whole[tap], (((1,), (1,)), ((), ())), preferred_element_type=F32
        )[offset : offset + rows]
        spread = product if spread is None else spread + product
    grad_input = (
        grad_hidden[EDGE : EDGE + rows].astype(F32) + spread * slope_first
    ).astype(BF16)

    total_first, grad_input = together(total_first, grad_input)
    across_first = across_y(total_first)
    across_second = across_y(line_sum(plane_second, line_second))
    done = finish(*together(*across_first, *across_second))
    return (tower[None], grad_input[None], done[0], done[1])


def solution(mesh):
    return jax.shard_map(
        shards,
        mesh=mesh,
        in_specs=(P("dp", "seq", None), P("dp", None), P("dp", None), P("dp", "seq", None)),
        out_specs=(P("dp", "seq", None), P("dp", "seq", None), P("dp", None), P("dp", None)),
        check_vma=False,
    )
```

```python
import math

import jax
import jax.numpy as jnp
from jax import lax
from jax.sharding import PartitionSpec as P

F32 = jnp.float32
BF16 = jnp.bfloat16
HALO = 16
EDGE = 8


def gelu_value(values):
    return values * 0.5 * (1.0 + lax.erf(values * 0.7071067811865476))


def gelu_slope(values):
    cumulative = 0.5 * (1.0 + lax.erf(values * 0.7071067811865476))
    density = jnp.exp(-0.5 * values * values) * 0.3989422804014327
    return cumulative + values * density


def together(*values):
    return lax.optimization_barrier(values)


def after(value, *others):
    return lax.optimization_barrier((value,) + others)[0]


def shards(features, w_first, w_second, cotangent):
    parts = lax.axis_size("dp")
    seqs = lax.axis_size("seq")
    place, me_y = lax.axis_index("dp"), lax.axis_index("seq")
    depth = parts // 4
    core, me_x, me_z = place % 2, (place // 2) % 2, place // 4
    h = me_y % 2
    rows, channels = features.shape[1], features.shape[2]
    block = w_first.shape[0]
    half = channels // 2
    grad_scale = 1.0 / math.sqrt(rows * seqs * parts)

    core_pairs = [(i, i ^ 1) for i in range(parts)]
    x_pairs = [(i, i ^ 2) for i in range(parts)]
    y_pairs = [(i, i ^ 1) for i in range(seqs)]

    def turn(step):
        return [(i, (i - 4 * step) % parts) for i in range(parts)]

    def by_core(mine, theirs, axis):
        first = jnp.where(core == 0, mine, theirs)
        second = jnp.where(core == 0, theirs, mine)
        return jnp.concatenate([first, second], axis=axis)

    def half_of(array, index, axis):
        return lax.dynamic_slice_in_dim(array, index * half, half, axis=axis)

    def take(array, index, axis):
        return lax.dynamic_index_in_dim(array, index, axis, keepdims=False)

    both = jnp.stack([w_first, w_second])
    given = lax.ppermute(half_of(both, 1 - core, 2), "dp", core_pairs)
    kept = half_of(both, core, 2)
    pair = jnp.stack(
        [jnp.where(core == 0, kept, given), jnp.where(core == 0, given, kept)], axis=1
    )

    joined = jnp.concatenate([features[0], cotangent[0]], axis=1)
    joined, pair = together(joined, pair)
    if seqs == 2:
        rim = jnp.where(h == 0, joined[rows - HALO :], joined[:HALO])
        rim = lax.ppermute(rim, "seq", y_pairs)
        none = jnp.zeros_like(rim)
        low, high = jnp.where(h == 0, none, rim), jnp.where(h == 0, rim, none)
    else:
        onward = [(i, i + 1) for i in range(seqs - 1)]
        back = [(i + 1, i) for i in range(seqs - 1)]
        low = lax.ppermute(joined[rows - HALO :], "seq", onward)
        high = lax.ppermute(joined[:HALO], "seq", back)

    def by_x(array):
        return lax.ppermute(array, "dp", x_pairs)

    def by_y(array):
        return lax.ppermute(array, "seq", y_pairs)

    def by_z(outs):
        return tuple(lax.ppermute(out, "dp", turn(step)) for step, out in enumerate(outs, 1))

    def along_z(piece):
        return jnp.stack(together(*by_z([piece] * (depth - 1))))

    def assemble(own, across, turned, from_x, from_y, from_xy):
        def on(flag, here, there, axis):
            return jnp.stack(
                [jnp.where(flag == 0, here, there), jnp.where(flag == 0, there, here)], axis=axis
            )

        near, far = on(h, turned, from_y, 1), on(h, from_x, from_xy, 1)
        near = jnp.concatenate([own[None], near], axis=0)
        far = jnp.concatenate([across[None], far], axis=0)
        lines = on(me_x, near, far, 1)
        lines = jnp.concatenate([lines, lines], axis=0)
        lines = lax.dynamic_slice_in_dim(lines, (depth - me_z) % depth, depth, axis=0)
        return lines.reshape(parts * block, half)

    first_piece, second_piece = (take(pair[which], h, 0) for which in range(2))
    first_turned, x_pair = together(along_z(first_piece), by_x(pair))
    low, high, second_piece = together(low, high, second_piece)
    second_turned = along_z(second_piece)
    first_x, first_y = by_x(first_turned), by_y(first_turned)
    first_x, first_y, second_turned = together(first_x, first_y, second_turned)
    second_x, second_y = by_x(second_turned), by_y(second_turned)
    first_pieces = pair[0], x_pair[0], first_turned, first_x, first_y, by_y(first_x)
    second_pieces = pair[1], x_pair[1], second_turned, second_x, second_y, by_x(second_y)

    extended = jnp.concatenate([low, joined, high], axis=0)
    partner = lax.ppermute(extended, "dp", core_pairs)
    pairs = jnp.stack([extended, partner])
    features_two, cot_two = pairs[..., :channels], pairs[..., channels:]
    act_first = gelu_value(features_two.astype(F32)).astype(BF16)
    wide = rows + 2 * EDGE

    def shifted(array, offset, count):
        return lax.slice_in_dim(array, offset, offset + count, axis=1)

    stack_first = jnp.concatenate(
        [shifted(act_first, HALO - EDGE + (tap - 1) * 4, wide) for tap in range(3)], axis=2
    )
    cot_mine = half_of(cot_two, core, 2)
    cot_base = shifted(cot_mine, HALO - EDGE, wide)
    row = lax.broadcasted_iota(jnp.int32, (1, wide, 1), 1)
    valid = (row >= jnp.where(me_y == 0, EDGE, 0)) & (
        row < jnp.where(me_y == seqs - 1, wide - EDGE, wide)
    )
    slope_first = gelu_slope(features[0].astype(F32))

    first_base = shifted(half_of(features_two, core, 2), HALO - EDGE, wide)
    first_mine = assemble(*first_pieces)
    first_theirs = lax.ppermute(first_mine, "dp", core_pairs)
    hidden = (
        first_base.astype(F32) + jnp.dot(stack_first, first_mine, preferred_element_type=F32)
    ).astype(BF16)
    act_mine = jnp.where(valid, gelu_value(hidden.astype(F32)), 0.0).astype(BF16)
    second_mine = assemble(*second_pieces)
    second_theirs = lax.ppermute(second_mine, "dp", core_pairs)
    act_theirs = lax.ppermute(act_mine, "dp", core_pairs)[::-1]
    act_second = by_core(act_mine, act_theirs, 2)
    stack_second = jnp.concatenate(
        [shifted(act_second, EDGE + (tap - 1) * 8, rows) for tap in range(3)], axis=2
    )

    def gradient(stacked, upstream):
        return (
            lax.dot_general(
                stacked.reshape(2 * rows, 3 * channels),
                upstream.reshape(2 * rows, half),
                (((0,), (0,)), ((), ())),
                preferred_element_type=F32,
            )
            * grad_scale
        ).astype(BF16)

    def add(left, right):
        return (left.astype(F32) + right.astype(F32)).astype(BF16)

    cut = depth // 2

    def first_out(grad):
        grad = grad.reshape(depth, 2, 2, block, half)
        return take(grad[:cut], 1 - me_x, 1), take(grad[cut:], 1 - h, 2)

    def first_sum(grad, one_in, two_in):
        grad = grad.reshape(depth, 2, 2, block, half)
        return add(take(grad[:cut], me_x, 1), one_in), add(take(grad[cut:], h, 2), two_in)

    def second_out(one, two):
        return take(one, 1 - h, 1), take(two, 1 - me_x, 1)

    def second_sum(one, two, one_in, two_in):
        one, two = add(take(one, h, 1), one_in), add(take(two, me_x, 1), two_in)
        return jnp.concatenate([one, two], axis=0)

    def line_out(summed):
        return tuple(take(summed, (me_z - step) % depth, 0) for step in range(1, depth))

    def line_sum(summed, came):
        total = take(summed, me_z, 0).astype(F32)
        for part in came:
            total = total + part.astype(F32)
        return total

    def across_y(total):
        if seqs > 2:
            groups = [[i for i in range(seqs) if i % 2 == k] for k in range(2)]
            total = lax.psum(total, "seq", axis_index_groups=groups)
        mine = total.astype(BF16)
        return mine, by_y(mine)

    def finish(*pieces):
        mine, theirs = pieces[::2], pieces[1::2]
        same = h == core
        given = jnp.stack([jnp.where(same, *pair) for pair in zip(theirs, mine)])
        given = lax.ppermute(given, "dp", core_pairs).astype(F32)
        kept = [jnp.where(same, *pair).astype(F32) for pair in zip(mine, theirs)]
        return [
            lax.dynamic_update_slice_in_dim(
                jnp.concatenate([own, own], axis=1), came, (1 - core) * half, axis=1
            )
            for own, came in zip(kept, given)
        ]

    slope = gelu_slope(hidden.astype(F32))
    mine, theirs = (
        take(side.reshape(3, 2, half, half), core, 1) for side in (second_mine, second_theirs)
    )
    product = lax.dot_general(
        cot_two,
        by_core(mine, theirs, 2).reshape(3 * half, channels),
        (((2,), (1,)), ((), ())),
        preferred_element_type=F32,
    )
    spread = None
    for tap in range(3):
        part = shifted(product[..., tap * half : (tap + 1) * half], HALO - EDGE - (tap - 1) * 8, wide)
        spread = part if spread is None else spread + part
    grad_mine = jnp.where(valid, cot_base.astype(F32) + spread * slope, 0.0).astype(BF16)
    grad_first = gradient(
        shifted(stack_first, EDGE, rows), shifted(grad_mine, EDGE, rows)
    )
    x_out, y_out = together(*first_out(grad_first))
    first_came = by_x(x_out), by_y(y_out)
    grad_second = gradient(stack_second, shifted(cot_mine, HALO, rows))

    tower_mine = (
        shifted(hidden, EDGE, rows).astype(F32)
        + jnp.dot(stack_second, second_mine, preferred_element_type=F32)
    ).astype(BF16)
    sent = jnp.concatenate([tower_mine[1], grad_mine[1]], axis=0)
    sent, grad_second = together(sent, grad_second)
    came = lax.ppermute(sent, "dp", core_pairs)
    came, *first_came = together(came, *first_came)
    half_first = first_sum(grad_first, *first_came)
    x_next, y_next = together(*first_out(grad_second))
    y_out, x_out = together(*second_out(*half_first))
    y_in, x_in, x_come, y_come = together(by_y(y_out), by_x(x_out), by_x(x_next), by_y(y_next))
    plane_first = second_sum(*half_first, y_in, x_in)
    half_second = first_sum(grad_second, x_come, y_come)
    y_out, x_out, *outs = together(*second_out(*half_second), *line_out(plane_first))
    total_first = line_sum(plane_first, together(*by_z(outs)))
    y_in, x_in, total_first = together(by_y(y_out), by_x(x_out), total_first)
    plane_second = second_sum(*half_second, y_in, x_in)
    total_first, *outs = together(total_first, *line_out(plane_second))
    line_second = by_z(outs)
    tower = by_core(tower_mine[0], came[:rows], 1)
    grad_hidden = by_core(grad_mine[0], came[rows:], 1)

    w_first_whole = by_core(first_mine, first_theirs, 1).reshape(3, channels, channels)
    spread = None
    for tap in range(3):
        offset = EDGE - (tap - 1) * 4
        product = lax.dot_general(
            grad_hidden, w_first_whole[tap], (((1,), (1,)), ((), ())), preferred_element_type=F32
        )[offset : offset + rows]
        spread = product if spread is None else spread + product
    grad_input = (
        grad_hidden[EDGE : EDGE + rows].astype(F32) + spread * slope_first
    ).astype(BF16)

    total_first, grad_input = together(total_first, grad_input)
    across_first = across_y(total_first)
    across_second = across_y(line_sum(plane_second, line_second))
    done = finish(*together(*across_first, *across_second))
    return (tower[None], grad_input[None], done[0], done[1])


def solution(mesh):
    return jax.shard_map(
        shards,
        mesh=mesh,
        in_specs=(P("dp", "seq", None), P("dp", None), P("dp", None), P("dp", "seq", None)),
        out_specs=(P("dp", "seq", None), P("dp", "seq", None), P("dp", None), P("dp", None)),
        check_vma=False,
    )
```

```python
import math

import jax
import jax.numpy as jnp
from jax import lax
from jax.sharding import PartitionSpec as P

F32 = jnp.float32
BF16 = jnp.bfloat16
HALO = 16
EDGE = 8


def gelu_value(values):
    return values * 0.5 * (1.0 + lax.erf(values * 0.7071067811865476))


def gelu_slope(values):
    cumulative = 0.5 * (1.0 + lax.erf(values * 0.7071067811865476))
    density = jnp.exp(-0.5 * values * values) * 0.3989422804014327
    return cumulative + values * density


def together(*values):
    return lax.optimization_barrier(values)


def after(value, *others):
    return lax.optimization_barrier((value,) + others)[0]


def shards(features, w_first, w_second, cotangent):
    parts = lax.axis_size("dp")
    seqs = lax.axis_size("seq")
    place, me_y = lax.axis_index("dp"), lax.axis_index("seq")
    depth = parts // 4
    core, me_x, me_z = place % 2, (place // 2) % 2, place // 4
    h = me_y % 2
    rows, channels = features.shape[1], features.shape[2]
    block = w_first.shape[0]
    half = channels // 2
    grad_scale = 1.0 / math.sqrt(rows * seqs * parts)

    core_pairs = [(i, i ^ 1) for i in range(parts)]
    x_pairs = [(i, i ^ 2) for i in range(parts)]
    y_pairs = [(i, i ^ 1) for i in range(seqs)]

    def turn(step):
        return [(i, (i - 4 * step) % parts) for i in range(parts)]

    def by_core(mine, theirs, axis):
        first = jnp.where(core == 0, mine, theirs)
        second = jnp.where(core == 0, theirs, mine)
        return jnp.concatenate([first, second], axis=axis)

    def half_of(array, index, axis):
        return lax.dynamic_slice_in_dim(array, index * half, half, axis=axis)

    def take(array, index, axis):
        return lax.dynamic_index_in_dim(array, index, axis, keepdims=False)

    both = jnp.stack([w_first, w_second])
    given = lax.ppermute(half_of(both, 1 - core, 2), "dp", core_pairs)
    kept = half_of(both, core, 2)
    pair = jnp.stack(
        [jnp.where(core == 0, kept, given), jnp.where(core == 0, given, kept)], axis=1
    )

    joined = jnp.concatenate([features[0], cotangent[0]], axis=1)
    joined, pair = together(joined, pair)
    if seqs == 2:
        rim = jnp.where(h == 0, joined[rows - HALO :], joined[:HALO])
        rim = lax.ppermute(rim, "seq", y_pairs)
        none = jnp.zeros_like(rim)
        low, high = jnp.where(h == 0, none, rim), jnp.where(h == 0, rim, none)
    else:
        onward = [(i, i + 1) for i in range(seqs - 1)]
        back = [(i + 1, i) for i in range(seqs - 1)]
        low = lax.ppermute(joined[rows - HALO :], "seq", onward)
        high = lax.ppermute(joined[:HALO], "seq", back)

    def by_x(array):
        return lax.ppermute(array, "dp", x_pairs)

    def by_y(array):
        return lax.ppermute(array, "seq", y_pairs)

    def by_z(outs):
        return tuple(lax.ppermute(out, "dp", turn(step)) for step, out in enumerate(outs, 1))

    def along_z(piece):
        return jnp.stack(together(*by_z([piece] * (depth - 1))))

    def assemble(own, across, turned, from_x, from_y, from_xy):
        def on(flag, here, there, axis):
            return jnp.stack(
                [jnp.where(flag == 0, here, there), jnp.where(flag == 0, there, here)], axis=axis
            )

        near, far = on(h, turned, from_y, 1), on(h, from_x, from_xy, 1)
        near = jnp.concatenate([own[None], near], axis=0)
        far = jnp.concatenate([across[None], far], axis=0)
        lines = on(me_x, near, far, 1)
        lines = jnp.concatenate([lines, lines], axis=0)
        lines = lax.dynamic_slice_in_dim(lines, (depth - me_z) % depth, depth, axis=0)
        return lines.reshape(parts * block, half)

    first_piece, second_piece = (take(pair[which], h, 0) for which in range(2))
    first_turned, x_pair = together(along_z(first_piece), by_x(pair))
    low, high, second_piece = together(low, high, second_piece)
    second_turned = along_z(second_piece)
    first_x, first_y = by_x(first_turned), by_y(first_turned)
    first_x, first_y, second_turned = together(first_x, first_y, second_turned)
    second_x, second_y = by_x(second_turned), by_y(second_turned)
    first_pieces = pair[0], x_pair[0], first_turned, first_x, first_y, by_y(first_x)
    second_pieces = pair[1], x_pair[1], second_turned, second_x, second_y, by_x(second_y)

    extended = jnp.concatenate([low, joined, high], axis=0)
    partner = lax.ppermute(extended, "dp", core_pairs)
    pairs = jnp.stack([extended, partner])
    features_two, cot_two = pairs[..., :channels], pairs[..., channels:]
    act_first = gelu_value(features_two.astype(F32)).astype(BF16)
    wide = rows + 2 * EDGE

    def shifted(array, offset, count):
        return lax.slice_in_dim(array, offset, offset + count, axis=1)

    stack_first = jnp.concatenate(
        [shifted(act_first, HALO - EDGE + (tap - 1) * 4, wide) for tap in range(3)], axis=2
    )
    cot_mine = half_of(cot_two, core, 2)
    cot_base = shifted(cot_mine, HALO - EDGE, wide)
    row = lax.broadcasted_iota(jnp.int32, (1, wide, 1), 1)
    valid = (row >= jnp.where(me_y == 0, EDGE, 0)) & (
        row < jnp.where(me_y == seqs - 1, wide - EDGE, wide)
    )
    slope_first = gelu_slope(features[0].astype(F32))

    first_base = shifted(half_of(features_two, core, 2), HALO - EDGE, wide)
    first_mine = assemble(*first_pieces)
    first_theirs = lax.ppermute(first_mine, "dp", core_pairs)
    hidden = (
        first_base.astype(F32) + jnp.dot(stack_first, first_mine, preferred_element_type=F32)
    ).astype(BF16)
    act_mine = jnp.where(valid, gelu_value(hidden.astype(F32)), 0.0).astype(BF16)
    second_mine = assemble(*second_pieces)
    second_theirs = lax.ppermute(second_mine, "dp", core_pairs)
    act_theirs = lax.ppermute(act_mine, "dp", core_pairs)[::-1]
    act_second = by_core(act_mine, act_theirs, 2)
    stack_second = jnp.concatenate(
        [shifted(act_second, EDGE + (tap - 1) * 8, rows) for tap in range(3)], axis=2
    )

    def gradient(stacked, upstream):
        return (
            lax.dot_general(
                stacked.reshape(2 * rows, 3 * channels),
                upstream.reshape(2 * rows, half),
                (((0,), (0,)), ((), ())),
                preferred_element_type=F32,
            )
            * grad_scale
        ).astype(BF16)

    def add(left, right):
        return (left.astype(F32) + right.astype(F32)).astype(BF16)

    cut = depth // 2

    def first_out(grad):
        grad = grad.reshape(depth, 2, 2, block, half)
        return take(grad[:cut], 1 - me_x, 1), take(grad[cut:], 1 - h, 2)

    def first_sum(grad, one_in, two_in):
        grad = grad.reshape(depth, 2, 2, block, half)
        return add(take(grad[:cut], me_x, 1), one_in), add(take(grad[cut:], h, 2), two_in)

    def second_out(one, two):
        return take(one, 1 - h, 1), take(two, 1 - me_x, 1)

    def second_sum(one, two, one_in, two_in):
        one, two = add(take(one, h, 1), one_in), add(take(two, me_x, 1), two_in)
        return jnp.concatenate([one, two], axis=0)

    def line_out(summed):
        return tuple(take(summed, (me_z - step) % depth, 0) for step in range(1, depth))

    def line_sum(summed, came):
        total = take(summed, me_z, 0).astype(F32)
        for part in came:
            total = total + part.astype(F32)
        return total

    def across_y(total):
        if seqs > 2:
            groups = [[i for i in range(seqs) if i % 2 == k] for k in range(2)]
            total = lax.psum(total, "seq", axis_index_groups=groups)
        mine = total.astype(BF16)
        return mine, by_y(mine)

    def finish(*pieces):
        mine, theirs = pieces[::2], pieces[1::2]
        same = h == core
        given = jnp.stack([jnp.where(same, *pair) for pair in zip(theirs, mine)])
        given = lax.ppermute(given, "dp", core_pairs).astype(F32)
        kept = [jnp.where(same, *pair).astype(F32) for pair in zip(mine, theirs)]
        return [
            lax.dynamic_update_slice_in_dim(
                jnp.concatenate([own, own], axis=1), came, (1 - core) * half, axis=1
            )
            for own, came in zip(kept, given)
        ]

    slope = gelu_slope(hidden.astype(F32))
    mine, theirs = (
        take(side.reshape(3, 2, half, half), core, 1) for side in (second_mine, second_theirs)
    )
    product = lax.dot_general(
        cot_two,
        by_core(mine, theirs, 2).reshape(3 * half, channels),
        (((2,), (1,)), ((), ())),
        preferred_element_type=F32,
    )
    spread = None
    for tap in range(3):
        part = shifted(product[..., tap * half : (tap + 1) * half], HALO - EDGE - (tap - 1) * 8, wide)
        spread = part if spread is None else spread + part
    grad_mine = jnp.where(valid, cot_base.astype(F32) + spread * slope, 0.0).astype(BF16)
    grad_first = gradient(
        shifted(stack_first, EDGE, rows), shifted(grad_mine, EDGE, rows)
    )
    x_out, y_out = together(*first_out(grad_first))
    first_came = by_x(x_out), by_y(y_out)
    grad_second = gradient(stack_second, shifted(cot_mine, HALO, rows))

    tower_mine = (
        shifted(hidden, EDGE, rows).astype(F32)
        + jnp.dot(stack_second, second_mine, preferred_element_type=F32)
    ).astype(BF16)
    sent, grad_second = together(grad_mine[1], grad_second)
    tower_came = lax.ppermute(tower_mine[1], "dp", core_pairs)
    came = lax.ppermute(sent, "dp", core_pairs)
    came, *first_came = together(came, *first_came)
    half_first = first_sum(grad_first, *first_came)
    x_next, y_next = together(*first_out(grad_second))
    y_out, x_out = together(*second_out(*half_first))
    y_in, x_in, x_come, y_come, tower_came = together(
        by_y(y_out), by_x(x_out), by_x(x_next), by_y(y_next), tower_came
    )
    plane_first = second_sum(*half_first, y_in, x_in)
    half_second = first_sum(grad_second, x_come, y_come)
    y_out, x_out, *outs = together(*second_out(*half_second), *line_out(plane_first))
    total_first = line_sum(plane_first, together(*by_z(outs)))
    y_in, x_in, total_first = together(by_y(y_out), by_x(x_out), total_first)
    plane_second = second_sum(*half_second, y_in, x_in)
    total_first, *outs = together(total_first, *line_out(plane_second))
    line_second = by_z(outs)
    tower = by_core(tower_mine[0], tower_came, 1)
    grad_hidden = by_core(grad_mine[0], came, 1)

    w_first_whole = by_core(first_mine, first_theirs, 1).reshape(3, channels, channels)
    spread = None
    for tap in range(3):
        offset = EDGE - (tap - 1) * 4
        product = lax.dot_general(
            grad_hidden, w_first_whole[tap], (((1,), (1,)), ((), ())), preferred_element_type=F32
        )[offset : offset + rows]
        spread = product if spread is None else spread + product
    grad_input = (
        grad_hidden[EDGE : EDGE + rows].astype(F32) + spread * slope_first
    ).astype(BF16)

    total_first, grad_input = together(total_first, grad_input)
    across_first = across_y(total_first)
    across_second = across_y(line_sum(plane_second, line_second))
    done = finish(*together(*across_first, *across_second))
    return (tower[None], grad_input[None], done[0], done[1])


def solution(mesh):
    return jax.shard_map(
        shards,
        mesh=mesh,
        in_specs=(P("dp", "seq", None), P("dp", None), P("dp", None), P("dp", "seq", None)),
        out_specs=(P("dp", "seq", None), P("dp", "seq", None), P("dp", None), P("dp", None)),
        check_vma=False,
    )
```
